32 devices in a mesh: gz: 8 (over y, x, core), gx: 4 (over z).
Axes of the slice: x: 2, y: 2, z: 4, core: 2. Of those that a mesh axis runs over, the one named last changes fastest.
Arguments:
- field_x: float32 [256, 128, 256], P('gx', 'gz'), may hold values from -6 to 6
- field_y: float32 [256, 128, 256], P('gx', 'gz'), may hold values from -6 to 6
- density: float32 [256, 128, 256], P('gx', 'gz'), may hold values from -6 to 6
Outputs:
- new_x: float32 [256, 128, 256], P('gx', 'gz')
- new_y: float32 [256, 128, 256], P('gx', 'gz')
The draws below stay inside these ranges and needn't reach their ends.
All inputs are finite; a program needn't handle non-finite values.
Results may differ from the reference program's by a relative error of at most 0.000096.
Values sent between devices are 32-bit elements; how exact they have to be, the bound alone decides.
A program may use at most 128 MiB of HBM per device.

```python
import math
import jax
import jax.numpy as jnp

NY = 256
STEPS = 2
NX = 256
NZ = 128


def block_scale(stream_key, dims, cuts, least, top_value):
    def one(dim, shards_of):
        heights = jax.random.uniform(jax.random.fold_in(jax.random.fold_in(stream_key, 6), dim), (shards_of,), jnp.float32, least / len(cuts), top_value / len(cuts))
        return jnp.repeat(jnp.exp(heights), dims[dim] // shards_of).reshape((-1,) + (1,) * (len(dims) - dim - 1))

    factor_of = one(*cuts[0])
    for cut in cuts[1:]:
        factor_of = factor_of * one(*cut)
    return factor_of


def noise(rng, dims, spread, bound, cuts=(), held_as=jnp.bfloat16):
    array = jax.random.normal(rng, dims, jnp.float32) * spread
    if len(cuts) > 0:
        array = block_scale(rng, dims, cuts, -0.22, 0.18) * array
    return jnp.clip(array, min=-bound, max=bound).astype(held_as)


def setup_inputs(seed: int = 0) -> dict:
    streams_of = jax.random.split(jax.random.key(seed), 4)
    return {
        "field_x": noise(streams_of[0], (NX, NZ, NY), 1.0, 6.0, ((0, 4), (1, 8)), jnp.float32),
        "field_y": noise(streams_of[1], (NX, NZ, NY), 1.0, 6.0, ((0, 4), (1, 8)), jnp.float32),
        "density": noise(streams_of[2], (NX, NZ, NY), 1.0, 6.0, ((0, 4), (1, 8)), jnp.float32),
    }


BEND_SCALE = 0.5
HEUN_STEP = 0.3

def transverse(values):
    padded = jnp.pad(values, ((1, 1), (0, 0), (1, 1)))
    return padded[2:, :, 1:-1] + padded[:-2, :, 1:-1] + padded[1:-1, :, 2:] + padded[1:-1, :, :-2] - 4.0 * values

def rate(values, source, curvature, scaling):
    integrand = 0.5 * transverse(values) - source
    summed = jnp.cumsum(integrand, axis=1)
    behind = jnp.pad(values, ((0, 0), (1, 0), (0, 0)))[:, :-1, :]
    return scaling * summed + curvature[:, None, None] * (behind - values)

def reference(field_x, field_y, density):
    padded = jnp.pad(density, ((1, 1), (0, 0), (1, 1)))
    grad_x = 0.5 * (padded[2:, :, 1:-1] - padded[:-2, :, 1:-1])
    grad_y = 0.5 * (padded[1:-1, :, 2:] - padded[1:-1, :, :-2])
    position = jnp.arange(NX, dtype=jnp.float32)
    curvature = BEND_SCALE * (2.0 * (position + 0.5) / NX - 1.0)
    scaling = 1.0 / math.sqrt(NZ)
    results = []
    for values, source in ((field_x, grad_x), (field_y, grad_y)):
        for repeat in range(STEPS):
            first_rate = rate(values, source, curvature, scaling)
            middle = values + HEUN_STEP * first_rate
            second_rate = rate(middle, source, curvature, scaling)
            values = values + 0.5 * HEUN_STEP * (first_rate + second_rate)
        results.append(values)
    return (results[0], results[1])
```

```python
import functools
import math

import jax
import jax.numpy as jnp
from jax import lax
from jax.experimental import pallas as pl
from jax.experimental.pallas import tpu as pltpu
from jax.sharding import PartitionSpec as P

STEPS = 2
BEND_SCALE = 0.5
HEUN_STEP = 0.3
HALO = 4
ORDERS = 4
MESH = pl.DeviceIdType.MESH


def shifted(parts, order, distance):
    n = distance
    result = parts[order - 1]
    factor = None
    for back in range(1, order):
        factor = n if factor is None else factor * (n + (back - 1.0)) / back
        result = result + factor * parts[order - 1 - back]
    return result


def exchange_kernel(
    slabs, groups, x_ref, y_ref, r_ref, sums_ref, planes_ref, halo_ref,
    halo, whole, edge, local, total, arrived, final, outgoing,
    halo_send, halo_recv, edge_send, edge_recv, scan_send, scan_recv, last_send, last_recv,
):
    gx = lax.axis_index("gx")
    gz = lax.axis_index("gz")
    rows, depth, width = x_ref.shape
    bits = slabs.bit_length() - 1
    half = lax.rem(gz, 2)
    sibling = gz + 1 - 2 * half
    fields = (x_ref, y_ref, r_ref)

    def partner(bit):
        size = 1 << bit
        return gz + size - 2 * size * lax.rem(gz // size, 2)

    barrier = pltpu.get_barrier_semaphore()

    def greet(device):
        pl.semaphore_signal(barrier, inc=1, device_id=device, device_id_type=MESH)

    for bit in range(bits):
        greet((partner(bit), gx))
    other = gz + 2 * half - 1
    paired = (other >= 0) & (other < slabs)
    pl.when(paired)(lambda: greet((other, gx)))
    pl.when(gx > 0)(lambda: greet((gz, gx - 1)))
    pl.when(gx < groups - 1)(lambda: greet((gz, gx + 1)))
    peers = bits + paired.astype(jnp.int32) + (gx > 0).astype(jnp.int32) + (gx < groups - 1).astype(jnp.int32)
    pl.semaphore_wait(barrier, peers)

    def halo_copy(a, side):
        start = 0 if side == 0 else rows - HALO
        return pltpu.make_async_remote_copy(
            src_ref=fields[a].at[pl.ds(start, HALO)],
            dst_ref=halo.at[a, side],
            send_sem=halo_send.at[a, side],
            recv_sem=halo_recv.at[a, side],
            device_id=(gz, gx - 1 + 2 * side),
            device_id_type=MESH,
        )

    def halo_start(side):
        for a in range(3):
            halo_copy(a, side).start()

    def halo_land(side):
        for a in range(3):
            halo_copy(a, side).wait_recv()

    def halo_clear(side):
        halo[:, side] = jnp.zeros((3, HALO, depth, width), jnp.float32)

    pl.when(gx > 0)(lambda: halo_start(0))
    pl.when(gx < groups - 1)(lambda: halo_start(1))

    for a in range(3):
        for z in range(depth):
            whole[a, z, 0:rows, :] = fields[a][:, z, :]
    pl.when(gx < groups - 1)(lambda: halo_land(0))
    pl.when(gx == groups - 1)(lambda: halo_clear(0))
    pl.when(gx > 0)(lambda: halo_land(1))
    pl.when(gx == 0)(lambda: halo_clear(1))
    for a in range(3):
        for z in range(depth):
            both = jnp.concatenate([halo[a, 0, :, z, :], halo[a, 1, :, z, :]], axis=0)
            whole[a, z, rows : rows + 2 * HALO, :] = both
    halo_ref[...] = whole[:, :, rows : rows + 2 * HALO, :]

    def edge_copy(a):
        return pltpu.make_async_remote_copy(
            src_ref=whole.at[a, pl.ds(depth - HALO, HALO)],
            dst_ref=edge.at[a],
            send_sem=edge_send.at[a],
            recv_sem=edge_recv.at[a],
            device_id=(gz + 1, gx),
            device_id_type=MESH,
        )

    tiles = (rows + 2 * HALO) // 8

    def tile_sums(t, _):
        at = pl.ds(pl.multiple_of(t * 8, 8), 8)
        for a in range(3):
            for h in range(2):
                cols = slice(h * (width // 2), (h + 1) * (width // 2))
                acc = [jnp.zeros((8, width // 2), jnp.float32) for _ in range(ORDERS)]
                for z in range(depth):
                    step = whole[a, z, at, cols]
                    for m in range(ORDERS):
                        acc[m] = acc[m] + step
                        step = acc[m]
                for m in range(ORDERS):
                    local[h, m, a, at, :] = acc[m]
        return 0

    lax.fori_loop(0, tiles, tile_sums, 0)

    def scan_copy(stage, m):
        if stage == 0:
            source = local.at[1 - half, m]
        else:
            source = total.at[stage - 1, m]
        return pltpu.make_async_remote_copy(
            src_ref=source,
            dst_ref=arrived.at[stage, m],
            send_sem=scan_send.at[stage, m],
            recv_sem=scan_recv.at[stage, m],
            device_id=(partner(stage), gx),
            device_id_type=MESH,
        )

    def last_copy(m):
        return pltpu.make_async_remote_copy(
            src_ref=outgoing.at[m],
            dst_ref=final.at[m],
            send_sem=last_send.at[m],
            recv_sem=last_recv.at[m],
            device_id=(sibling, gx),
            device_id_type=MESH,
        )

    for m in range(ORDERS):
        scan_copy(0, m).start()
    pl.when(gz < slabs - 1)(lambda: [edge_copy(a).start() for a in range(3)] and None)

    is_odd = half.astype(jnp.float32)
    lower, upper = [], []
    for m in range(ORDERS):
        scan_copy(0, m).wait_recv()
        mine, theirs = local[half, m], arrived[0, m]
        low = jnp.where(half == 0, mine, theirs)
        lower.append(low)
        high = jnp.where(half == 0, theirs, mine)
        if bits > 1:
            total[0, m] = shifted(lower, m + 1, float(depth)) + high
            if bits == 2:
                pl.when(partner(1) > gz)(lambda: scan_copy(1, m).start())
            else:
                scan_copy(1, m).start()
    prefix = [jnp.zeros_like(local[0, 0])] * ORDERS
    for bit in range(1, bits):
        size = 1 << bit
        is_upper = lax.rem(gz // size, 2)
        last = bit == bits - 1
        span = float(depth * size)
        inside = lax.rem(gz, size) - half
        distance = (inside * depth).astype(jnp.float32)
        gate = is_upper.astype(jnp.float32)
        lows, adds = [], []
        for m in range(ORDERS):
            if last:
                pl.when(is_upper == 1)(lambda: scan_copy(bit, m).wait_recv())

                def clear():
                    arrived[bit, m] = jnp.zeros_like(arrived[bit, m])

                pl.when(is_upper == 0)(clear)
            else:
                scan_copy(bit, m).wait_recv()
            theirs = arrived[bit, m]
            adds.append(theirs)
            if not last:
                mine = total[bit - 1, m]
                lows.append(jnp.where(is_upper == 0, mine, theirs))
                high = jnp.where(is_upper == 0, theirs, mine)
                total[bit, m] = shifted(lows, m + 1, span) + high
                if bit + 1 == bits - 1:
                    pl.when(partner(bit + 1) > gz)(lambda: scan_copy(bit + 1, m).start())
                else:
                    scan_copy(bit + 1, m).start()
            prefix[m] = prefix[m] + gate * shifted(adds, m + 1, distance)
            if last:
                even = prefix[m]
                odd = shifted(prefix, m + 1, float(depth)) + lower[m]
                sums_ref[half, m] = jnp.where(half == 0, even, odd)
                outgoing[m] = jnp.where(half == 0, odd, even)
                last_copy(m).start()
    for m in range(ORDERS):
        last_copy(m).wait_recv()
        sums_ref[1 - half, m] = final[m]

    def edge_land():
        for a in range(3):
            edge_copy(a).wait_recv()
        planes_ref[...] = edge[...]

    def edge_clear():
        planes_ref[...] = jnp.zeros(planes_ref.shape, jnp.float32)

    pl.when(gz > 0)(edge_land)
    pl.when(gz == 0)(edge_clear)

    pl.when(gz < slabs - 1)(lambda: [edge_copy(a).wait_send() for a in range(3)] and None)
    pl.when(gx > 0)(lambda: [halo_copy(a, 0).wait_send() for a in range(3)] and None)
    pl.when(gx < groups - 1)(lambda: [halo_copy(a, 1).wait_send() for a in range(3)] and None)
    for m in range(ORDERS):
        last_copy(m).wait_send()
        for bit in range(bits):
            if bit == bits - 1:
                pl.when(partner(bit) > gz)(lambda: scan_copy(bit, m).wait_send())
            else:
                scan_copy(bit, m).wait_send()


def march_kernel(total_rows, scaling, x_ref, y_ref, r_ref, sums_ref, planes_ref, halo_ref, ox_ref, oy_ref, base, source, middle, rho):
    gx = lax.axis_index("gx")
    rows, depth, width = x_ref.shape
    tall = rows + 2 * HALO
    shape = (tall, width)
    row = lax.broadcasted_iota(jnp.int32, shape, 0)
    column = lax.broadcasted_iota(jnp.int32, shape, 1)
    place = gx * rows + jnp.where(row >= rows + HALO, row - tall, row)
    inside = ((place >= 0) & (place < total_rows)).astype(jnp.float32)
    curve = BEND_SCALE * (2.0 * (place.astype(jnp.float32) + 0.5) / total_rows - 1.0)
    curve = curve * inside

    def beside_y(v):
        up = jnp.where(column == width - 1, 0.0, pltpu.roll(v, width - 1, 1))
        down = jnp.where(column == 0, 0.0, pltpu.roll(v, 1, 1))
        return up, down

    def beside_x(v):
        return pltpu.roll(v, tall - 1, 0), pltpu.roll(v, 1, 0)

    half_scale = 0.5 * scaling

    def lap(v):
        up, down = beside_y(v)
        after, before = beside_x(v)
        return (half_scale * inside) * (after + before + up + down - 4.0 * v)

    def grad(f, v):
        one, two = beside_x(v) if f == 0 else beside_y(v)
        return (half_scale * inside) * (one - two)

    def plane_rate(f, planes, sources, m):
        return lap(planes[m + 1]) - sources[m + 1] - curve * planes[m - 1]

    for a, ref in enumerate((x_ref, y_ref, r_ref)):
        for z in range(depth):
            target = rho if a == 2 else base.at[a]
            target[z, 0:rows, :] = ref[:, z, :]
            target[z, rows:tall, :] = halo_ref[a, z]

    def make_source(z, _):
        v = rho[z]
        for f in range(2):
            source[f, z] = grad(f, v)
        return 0

    lax.fori_loop(0, depth, make_source, 0)

    def joined(m, a):
        return jnp.concatenate([sums_ref[0, m, a], sums_ref[1, m, a]], axis=1)

    density = {m: joined(m - 1, 2) for m in range(1, ORDERS + 1)}
    density[0] = planes_ref[2, 3]
    density[-1] = planes_ref[2, 3] - planes_ref[2, 2]
    heads = []
    for f in range(2):
        sources = {m: grad(f, v) for m, v in density.items()}
        first = {m: joined(m - 1, f) for m in range(1, ORDERS + 1)}
        p3, p2, p1, p0 = (planes_ref[f, i] for i in range(4))
        first[0] = p0
        first[-1] = p0 - p1
        first[-2] = p0 - 2.0 * p1 + p2
        first[-3] = p0 - 3.0 * (p1 - p2) - p3
        second = {m: first[m] + HEUN_STEP * plane_rate(f, first, sources, m) for m in range(-2, 4)}
        third = {
            m: 0.5 * (first[m] + second[m]) + 0.5 * HEUN_STEP * plane_rate(f, second, sources, m)
            for m in range(-1, 3)
        }
        fourth = {m: third[m] + HEUN_STEP * plane_rate(f, third, sources, m) for m in range(0, 2)}
        heads.append([(p[0], lap(p[1]) - sources[1]) for p in (first, second, third, fourth)])

    outs = (ox_ref, oy_ref)
    for f in range(2):
        for step in range(STEPS):
            def one(z, carry):
                behind, acc = carry
                v = base[f, z]
                acc = acc + lap(v) - source[f, z]
                middle[f, z] = v + HEUN_STEP * (acc + curve * (behind - v))
                return v, acc

            lax.fori_loop(0, depth, one, heads[f][2 * step])

            def two(z, carry):
                behind, acc = carry
                v = middle[f, z]
                acc = acc + lap(v) - source[f, z]
                rate = acc + curve * (behind - v)
                base[f, z] = 0.5 * (base[f, z] + v) + 0.5 * HEUN_STEP * rate
                return v, acc

            lax.fori_loop(0, depth, two, heads[f][2 * step + 1])
        for z in range(depth):
            outs[f][:, z, :] = base[f, z, 0:rows, :]


def shards(slabs, groups, field_x, field_y, density):
    rows, depth, width = field_x.shape
    tall = rows + 2 * HALO
    bits = slabs.bit_length() - 1
    f32 = jnp.float32
    vmem = pl.BlockSpec(memory_space=pltpu.VMEM)
    dma = pltpu.SemaphoreType.DMA
    chunk = (ORDERS, 3, tall, width // 2)
    sums, planes, halo = pl.pallas_call(
        functools.partial(exchange_kernel, slabs, groups),
        out_shape=(
            jax.ShapeDtypeStruct((2,) + chunk, f32),
            jax.ShapeDtypeStruct((3, HALO, tall, width), f32),
            jax.ShapeDtypeStruct((3, depth, 2 * HALO, width), f32),
        ),
        in_specs=[vmem] * 3,
        out_specs=[vmem] * 3,
        scratch_shapes=[
            pltpu.VMEM((3, 2, HALO, depth, width), f32),
            pltpu.VMEM((3, depth, tall, width), f32),
            pltpu.VMEM((3, HALO, tall, width), f32),
            pltpu.VMEM((2,) + chunk, f32),
            pltpu.VMEM((max(bits - 1, 1),) + chunk, f32),
            pltpu.VMEM((bits,) + chunk, f32),
            pltpu.VMEM(chunk, f32),
            pltpu.VMEM(chunk, f32),
            dma((3, 2)),
            dma((3, 2)),
            dma((3,)),
            dma((3,)),
            dma((bits, ORDERS)),
            dma((bits, ORDERS)),
            dma((ORDERS,)),
            dma((ORDERS,)),
        ],
        compiler_params=pltpu.CompilerParams(
            collective_id=0, has_side_effects=True, vmem_limit_bytes=48 * 1024 * 1024
        ),
        name="exchange",
    )(field_x, field_y, density)
    result = jax.ShapeDtypeStruct(field_x.shape, f32)
    return pl.pallas_call(
        functools.partial(march_kernel, rows * groups, 1.0 / math.sqrt(depth * slabs)),
        out_shape=(result, result),
        in_specs=[vmem] * 6,
        out_specs=[vmem] * 2,
        scratch_shapes=[
            pltpu.VMEM((2, depth, tall, width), f32),
            pltpu.VMEM((2, depth, tall, width), f32),
            pltpu.VMEM((2, depth, tall, width), f32),
            pltpu.VMEM((depth, tall, width), f32),
        ],
        compiler_params=pltpu.CompilerParams(vmem_limit_bytes=48 * 1024 * 1024),
        name="march",
    )(field_x, field_y, density, sums, planes, halo)


def solution(mesh):
    spec = P("gx", "gz", None)
    return jax.shard_map(
        functools.partial(shards, mesh.shape["gz"], mesh.shape["gx"]),
        mesh=mesh,
        in_specs=(spec, spec, spec),
        out_specs=(spec, spec),
        check_vma=False,
    )
```

```python
import functools
import math

import jax
import jax.numpy as jnp
from jax import lax
from jax.experimental import pallas as pl
from jax.experimental.pallas import tpu as pltpu
from jax.sharding import PartitionSpec as P

STEPS = 2
BEND_SCALE = 0.5
HEUN_STEP = 0.3
HALO = 4
ORDERS = 4
MESH = pl.DeviceIdType.MESH


def shifted(parts, order, distance):
    n = distance
    result = parts[order - 1]
    factor = None
    for back in range(1, order):
        factor = n if factor is None else factor * (n + (back - 1.0)) / back
        result = result + factor * parts[order - 1 - back]
    return result


def exchange_kernel(
    slabs, groups, depth, x_ref, y_ref, r_ref, sums_ref, planes_ref, halo_ref,
    ext, edge_out, edge, local, total, arrived, final, outgoing,
    own_sem, halo_send, halo_recv, edge_send, edge_recv, scan_send, scan_recv, last_send, last_recv,
):
    gx = lax.axis_index("gx")
    gz = lax.axis_index("gz")
    length, width = x_ref.shape
    w = width // 2
    margin = HALO * depth
    tiles = length // depth // 8 + 1
    fields = (x_ref, y_ref, r_ref)

    def own_copy(a, h):
        return pltpu.make_async_copy(
            fields[a].at[:, pl.ds(h * w, w)], ext.at[a, h, pl.ds(margin, length)], own_sem.at[a, h]
        )

    for a in range(3):
        for h in range(2):
            own_copy(a, h).start()

    bits = slabs.bit_length() - 1
    half = lax.rem(gz, 2)
    sibling = gz + 1 - 2 * half

    def partner(bit):
        size = 1 << bit
        return gz + size - 2 * size * lax.rem(gz // size, 2)

    barrier = pltpu.get_barrier_semaphore()

    def greet(device):
        pl.semaphore_signal(barrier, inc=1, device_id=device, device_id_type=MESH)

    for bit in range(bits):
        greet((partner(bit), gx))
    other = gz + 2 * half - 1
    paired = (other >= 0) & (other < slabs)
    pl.when(paired)(lambda: greet((other, gx)))
    pl.when(gx > 0)(lambda: greet((gz, gx - 1)))
    pl.when(gx < groups - 1)(lambda: greet((gz, gx + 1)))
    peers = bits + paired.astype(jnp.int32) + (gx > 0).astype(jnp.int32) + (gx < groups - 1).astype(jnp.int32)
    pl.semaphore_wait(barrier, peers)

    def halo_copy(a, side, h):
        return pltpu.make_async_remote_copy(
            src_ref=fields[a].at[pl.ds(0 if side == 0 else length - margin, margin), pl.ds(h * w, w)],
            dst_ref=ext.at[a, h, pl.ds(margin + length if side == 0 else 0, margin)],
            send_sem=halo_send.at[a, side, h],
            recv_sem=halo_recv.at[a, side, h],
            device_id=(gz, gx - 1 + 2 * side),
            device_id_type=MESH,
        )

    def halo_start(side):
        for a in range(3):
            for h in range(2):
                halo_copy(a, side, h).start()

    def halo_land(side):
        for a in range(3):
            for h in range(2):
                halo_copy(a, side, h).wait_recv()

    def halo_clear(side):
        ext[:, :, pl.ds(margin + length if side == 0 else 0, margin)] = jnp.zeros((3, 2, margin, w), jnp.float32)

    pl.when(gx > 0)(lambda: halo_start(0))
    pl.when(gx < groups - 1)(lambda: halo_start(1))
    for a in range(3):
        for h in range(2):
            own_copy(a, h).wait()
    pl.when(gx < groups - 1)(lambda: halo_land(0))
    pl.when(gx == groups - 1)(lambda: halo_clear(0))
    pl.when(gx > 0)(lambda: halo_land(1))
    pl.when(gx == 0)(lambda: halo_clear(1))

    def edge_copy():
        return pltpu.make_async_remote_copy(
            src_ref=edge_out,
            dst_ref=edge,
            send_sem=edge_send,
            recv_sem=edge_recv,
            device_id=(gz + 1, gx),
            device_id_type=MESH,
        )

    def tile_sums(t, _):
        for a in range(3):
            for h in range(2):
                acc = [jnp.zeros((8, w), jnp.float32) for _ in range(ORDERS)]
                for z in range(depth):
                    step = ext[a, h, pl.ds(t * depth + z, 8, stride=tiles * depth), :]
                    if a < 2 and z >= depth - 4:
                        edge_out[4 * a + z - (depth - 4), t, :, pl.ds(h * w, w)] = step
                    if a == 2 and z >= depth - 2:
                        edge_out[8 + z - (depth - 2), t, :, pl.ds(h * w, w)] = step
                    for m in range(ORDERS):
                        acc[m] = acc[m] + step
                        step = acc[m]
                for m in range(ORDERS):
                    local[h, m, a, t] = acc[m]
        return 0

    lax.fori_loop(0, tiles, tile_sums, 0)
    halo_ref[:, 0] = ext[:, :, 0:margin]
    halo_ref[:, 1] = ext[:, :, margin + length : 2 * margin + length]

    def scan_copy(stage, m):
        if stage == 0:
            source = local.at[1 - half, m]
        else:
            source = total.at[stage - 1, m]
        return pltpu.make_async_remote_copy(
            src_ref=source,
            dst_ref=arrived.at[stage, m],
            send_sem=scan_send.at[stage, m],
            recv_sem=scan_recv.at[stage, m],
            device_id=(partner(stage), gx),
            device_id_type=MESH,
        )

    def last_copy(m):
        return pltpu.make_async_remote_copy(
            src_ref=outgoing.at[m],
            dst_ref=final.at[m],
            send_sem=last_send.at[m],
            recv_sem=last_recv.at[m],
            device_id=(sibling, gx),
            device_id_type=MESH,
        )

    for m in range(ORDERS):
        scan_copy(0, m).start()
    pl.when(gz < slabs - 1)(lambda: edge_copy().start())

    is_odd = half.astype(jnp.float32)
    lower, upper = [], []
    for m in range(ORDERS):
        scan_copy(0, m).wait_recv()
        mine, theirs = local[half, m], arrived[0, m]
        low = jnp.where(half == 0, mine, theirs)
        lower.append(low)
        high = jnp.where(half == 0, theirs, mine)
        if bits > 1:
            total[0, m] = shifted(lower, m + 1, float(depth)) + high
            if bits == 2:
                pl.when(partner(1) > gz)(lambda: scan_copy(1, m).start())
            else:
                scan_copy(1, m).start()
    prefix = [jnp.zeros_like(local[0, 0])] * ORDERS
    for bit in range(1, bits):
        size = 1 << bit
        is_upper = lax.rem(gz // size, 2)
        last = bit == bits - 1
        span = float(depth * size)
        inside = lax.rem(gz, size) - half
        distance = (inside * depth).astype(jnp.float32)
        gate = is_upper.astype(jnp.float32)
        lows, adds = [], []
        for m in range(ORDERS):
            if last:
                pl.when(is_upper == 1)(lambda: scan_copy(bit, m).wait_recv())

                def clear():
                    arrived[bit, m] = jnp.zeros_like(arrived[bit, m])

                pl.when(is_upper == 0)(clear)
            else:
                scan_copy(bit, m).wait_recv()
            theirs = arrived[bit, m]
            adds.append(theirs)
            if not last:
                mine = total[bit - 1, m]
                lows.append(jnp.where(is_upper == 0, mine, theirs))
                high = jnp.where(is_upper == 0, theirs, mine)
                total[bit, m] = shifted(lows, m + 1, span) + high
                if bit + 1 == bits - 1:
                    pl.when(partner(bit + 1) > gz)(lambda: scan_copy(bit + 1, m).start())
                else:
                    scan_copy(bit + 1, m).start()
            prefix[m] = prefix[m] + gate * shifted(adds, m + 1, distance)
            if last:
                even = prefix[m]
                odd = shifted(prefix, m + 1, float(depth)) + lower[m]
                sums_ref[half, m] = jnp.where(half == 0, even, odd)
                outgoing[m] = jnp.where(half == 0, odd, even)
                last_copy(m).start()
    for m in range(ORDERS):
        last_copy(m).wait_recv()
        sums_ref[1 - half, m] = final[m]

    def edge_land():
        edge_copy().wait_recv()
        planes_ref[...] = edge[...]

    def edge_clear():
        planes_ref[...] = jnp.zeros(planes_ref.shape, jnp.float32)

    pl.when(gz > 0)(edge_land)
    pl.when(gz == 0)(edge_clear)

    pl.when(gz < slabs - 1)(lambda: edge_copy().wait_send())

    def halo_sent(side):
        for a in range(3):
            for h in range(2):
                halo_copy(a, side, h).wait_send()

    pl.when(gx > 0)(lambda: halo_sent(0))
    pl.when(gx < groups - 1)(lambda: halo_sent(1))
    for m in range(ORDERS):
        last_copy(m).wait_send()
        for bit in range(bits):
            if bit == bits - 1:
                pl.when(partner(bit) > gz)(lambda: scan_copy(bit, m).wait_send())
            else:
                scan_copy(bit, m).wait_send()


def march_kernel(
    total_rows, scaling, depth, x_ref, y_ref, r_ref, sums_ref, planes_ref, halo_ref, ox_ref, oy_ref,
    ext, base, middle, rho, source, density, pull, heads, own_sem,
):
    gx = lax.axis_index("gx")
    length, width = x_ref.shape
    margin = HALO * depth
    tiles = length // depth // 8 + 1
    w = width // 2
    fields = (x_ref, y_ref, r_ref)
    lane = lax.broadcasted_iota(jnp.int32, (8, w), 1)
    sub = lax.broadcasted_iota(jnp.int32, (8, w), 0)
    first_lane, last_lane = lane == 0, lane == w - 1

    def own_copy(a, h):
        return pltpu.make_async_copy(
            fields[a].at[:, pl.ds(h * w, w)], ext.at[a, h, pl.ds(margin, length)], own_sem.at[a, h]
        )

    for a in range(3):
        for h in range(2):
            own_copy(a, h).start()
    ext[:, :, 0:margin] = halo_ref[:, 0]
    ext[:, :, margin + length : 2 * margin + length] = halo_ref[:, 1]

    def coefficients(t):
        place = gx * (length // depth) - HALO + sub * tiles + t
        inside = ((place >= 0) & (place < total_rows)).astype(jnp.float32)
        curve = BEND_SCALE * (2.0 * (place.astype(jnp.float32) + 0.5) / total_rows - 1.0)
        return (0.5 * HEUN_STEP * scaling) * inside, HEUN_STEP * curve * inside

    def halves(v):
        return [v[:, :w], v[:, w:]]

    def beside_y(v):
        a, b = v
        ua, ub = pltpu.roll(a, w - 1, 1), pltpu.roll(b, w - 1, 1)
        da, db = pltpu.roll(a, 1, 1), pltpu.roll(b, 1, 1)
        up = [jnp.where(last_lane, ub, ua), jnp.where(last_lane, 0.0, ub)]
        down = [jnp.where(first_lane, 0.0, da), jnp.where(first_lane, da, db)]
        return up, down

    def wrap(ref, *index):
        ref[(*index, 0)] = pltpu.roll(ref[(*index, tiles)], 1, 0)
        ref[(*index, tiles + 1)] = pltpu.roll(ref[(*index, 1)], 7, 0)

    def laplace(ref, index, t):
        v = halves(ref[(*index, t + 1)])
        before, after = halves(ref[(*index, t)]), halves(ref[(*index, t + 2)])
        up, down = beside_y(v)
        return v, [(b + a) + (u + d) - 4.0 * c for a, b, c, u, d in zip(after, before, v, up, down)]

    def gradients(ref, index, t):
        v = halves(ref[(*index, t + 1)])
        before, after = halves(ref[(*index, t)]), halves(ref[(*index, t + 2)])
        up, down = beside_y(v)
        return [[a - b for a, b in zip(after, before)], [u - d for u, d in zip(up, down)]]

    def put(ref, index, value):
        ref[(*index, slice(None), slice(0, w))] = value[0]
        ref[(*index, slice(None), slice(w, width))] = value[1]

    low, high = (-3, -2, -1, 0), (4, 3, 2, 1)
    first = (0, 8, 14, 18)

    def at(n, m):
        return first[n] + m - low[n]

    def load_heads(t, _):
        for m in range(1, ORDERS + 1):
            for f in range(2):
                put(heads, (f, at(0, m), t + 1), [sums_ref[0, m - 1, f, t], sums_ref[1, m - 1, f, t]])
            put(density, (m + 1, t + 1), [sums_ref[0, m - 1, 2, t], sums_ref[1, m - 1, 2, t]])
        for f in range(2):
            p3, p2, p1, p0 = (planes_ref[4 * f + i, t] for i in range(4))
            heads[f, at(0, 0), t + 1] = p0
            heads[f, at(0, -1), t + 1] = p0 - p1
            heads[f, at(0, -2), t + 1] = p0 - 2.0 * p1 + p2
            heads[f, at(0, -3), t + 1] = p0 - 3.0 * (p1 - p2) - p3
        density[1, t + 1] = planes_ref[9, t]
        density[0, t + 1] = planes_ref[9, t] - planes_ref[8, t]
        return 0

    lax.fori_loop(0, tiles, load_heads, 0)
    for i in range(ORDERS + 2):
        wrap(density, i)
    for f in range(2):
        for i in range(8):
            wrap(heads, f, i)

    def pull_tile(t, _):
        for i in range(ORDERS + 2):
            for f, g in enumerate(gradients(density, (i,), t)):
                put(pull, (f, i, t), g)
        return 0

    lax.fori_loop(0, tiles, pull_tile, 0)

    for n in range(1, 4):
        def raise_tile(t, _, n=n):
            c, k = coefficients(t)
            for f in range(2):
                for m in range(low[n], high[n] + 1):
                    _, force = laplace(heads, (f, at(n - 1, m + 1)), t)
                    g = halves(pull[f, m + 2, t])
                    now = halves(heads[f, at(n - 1, m), t + 1])
                    less = halves(heads[f, at(n - 1, m - 1), t + 1])
                    new = [v + c * (q - s) - k * d for v, q, s, d in zip(now, force, g, less)]
                    if n == 2:
                        old = halves(heads[f, at(0, m), t + 1])
                        new = [0.5 * (o + e) for o, e in zip(old, new)]
                    put(heads, (f, at(n, m), t + 1), new)
            return 0

        lax.fori_loop(0, tiles, raise_tile, 0)
        for f in range(2):
            for m in range(low[n], high[n] + 1):
                wrap(heads, f, at(n, m))

    for a in range(3):
        for h in range(2):
            own_copy(a, h).wait()

    def spread(t, _):
        for a in range(3):
            for z in range(depth):
                rows = pl.ds(t * depth + z, 8, stride=tiles * depth)
                v = [ext[a, h, rows, :] for h in range(2)]
                if a == 2:
                    put(rho, (z, t + 1), v)
                else:
                    put(base, (a, z, t + 1), v)
        return 0

    lax.fori_loop(0, tiles, spread, 0)
    for z in range(depth):
        wrap(rho, z)
        wrap(base, 0, z)
        wrap(base, 1, z)

    def source_tile(t, _):
        for z in range(depth):
            for f, g in enumerate(gradients(rho, (z,), t)):
                put(source, (f, z, t), g)
        return 0

    lax.fori_loop(0, tiles, source_tile, 0)

    def out_copy(f, h):
        return pltpu.make_async_copy(
            ext.at[f, h, pl.ds(margin, length)], (ox_ref, oy_ref)[f].at[:, pl.ds(h * w, w)], own_sem.at[f, h]
        )

    for f in range(2):
        for n in range(2 * STEPS):
            origin, target = (base, middle) if n % 2 == 0 else (middle, base)

            def level_tile(t, _, f=f, n=n, origin=origin, target=target):
                c, k = coefficients(t)
                _, acc = laplace(heads, (f, at(n, 1)), t)
                acc = [q - s for q, s in zip(acc, halves(pull[f, 2, t]))]
                behind = halves(heads[f, at(n, 0), t + 1])
                for z in range(depth):
                    v, force = laplace(origin, (f, z), t)
                    g = halves(source[f, z, t])
                    acc = [p + (q - s) for p, q, s in zip(acc, force, g)]
                    new = [e + c * p + k * (b - e) for e, p, b in zip(v, acc, behind)]
                    if n % 2 == 1:
                        new = [0.5 * (o + e) for o, e in zip(halves(base[f, z, t + 1]), new)]
                    if n == 2 * STEPS - 1:
                        rows = pl.ds(t * depth + z, 8, stride=tiles * depth)
                        for h in range(2):
                            ext[f, h, rows, :] = new[h]
                    else:
                        put(target, (f, z, t + 1), new)
                    behind = v
                return 0

            lax.fori_loop(0, tiles, level_tile, 0)
            if n < 2 * STEPS - 1:
                for z in range(depth):
                    wrap(target, f, z)
        for h in range(2):
            out_copy(f, h).start()
    for f in range(2):
        for h in range(2):
            out_copy(f, h).wait()


def shards(slabs, groups, field_x, field_y, density):
    rows, depth, width = field_x.shape
    tiles = rows // 8 + 1
    length, margin = rows * depth, HALO * depth
    bits = slabs.bit_length() - 1
    f32 = jnp.float32
    vmem = pl.BlockSpec(memory_space=pltpu.VMEM)
    anywhere = pl.BlockSpec(memory_space=pl.ANY)
    dma = pltpu.SemaphoreType.DMA
    chunk = (ORDERS, 3, tiles, 8, width // 2)
    args = [v.reshape(length, width) for v in (field_x, field_y, density)]
    sums, planes, halo = pl.pallas_call(
        functools.partial(exchange_kernel, slabs, groups, depth),
        out_shape=(
            jax.ShapeDtypeStruct((2,) + chunk, f32),
            jax.ShapeDtypeStruct((10, tiles, 8, width), f32),
            jax.ShapeDtypeStruct((3, 2, 2, margin, width // 2), f32),
        ),
        in_specs=[anywhere] * 3,
        out_specs=[vmem] * 3,
        scratch_shapes=[
            pltpu.VMEM((3, 2, length + 2 * margin, width // 2), f32),
            pltpu.VMEM((10, tiles, 8, width), f32),
            pltpu.VMEM((10, tiles, 8, width), f32),
            pltpu.VMEM((2,) + chunk, f32),
            pltpu.VMEM((max(bits - 1, 1),) + chunk, f32),
            pltpu.VMEM((bits,) + chunk, f32),
            pltpu.VMEM(chunk, f32),
            pltpu.VMEM(chunk, f32),
            dma((3, 2)),
            dma((3, 2, 2)),
            dma((3, 2, 2)),
            dma,
            dma,
            dma((bits, ORDERS)),
            dma((bits, ORDERS)),
            dma((ORDERS,)),
            dma((ORDERS,)),
        ],
        compiler_params=pltpu.CompilerParams(
            collective_id=0, has_side_effects=True, vmem_limit_bytes=48 * 1024 * 1024
        ),
        name="exchange",
    )(*args)
    result = jax.ShapeDtypeStruct((length, width), f32)
    plane = (tiles + 2, 8, width)
    new_x, new_y = pl.pallas_call(
        functools.partial(march_kernel, rows * groups, 1.0 / math.sqrt(depth * slabs), depth),
        out_shape=(result, result),
        in_specs=[anywhere] * 3 + [vmem] * 3,
        out_specs=[anywhere] * 2,
        scratch_shapes=[
            pltpu.VMEM((3, 2, length + 2 * margin, width // 2), f32),
            pltpu.VMEM((2, depth) + plane, f32),
            pltpu.VMEM((2, depth) + plane, f32),
            pltpu.VMEM((depth,) + plane, f32),
            pltpu.VMEM((2, depth, tiles, 8, width), f32),
            pltpu.VMEM((ORDERS + 2,) + plane, f32),
            pltpu.VMEM((2, ORDERS + 2, tiles, 8, width), f32),
            pltpu.VMEM((2, 20) + plane, f32),
            dma((3, 2)),
        ],
        compiler_params=pltpu.CompilerParams(vmem_limit_bytes=48 * 1024 * 1024),
        name="march",
    )(*args, sums, planes, halo)
    return new_x.reshape(field_x.shape), new_y.reshape(field_x.shape)


def solution(mesh):
    spec = P("gx", "gz", None)
    return jax.shard_map(
        functools.partial(shards, mesh.shape["gz"], mesh.shape["gx"]),
        mesh=mesh,
        in_specs=(spec, spec, spec),
        out_specs=(spec, spec),
        check_vma=False,
    )
```

```python
import functools
import math

import jax
import jax.numpy as jnp
from jax import lax
from jax.experimental import pallas as pl
from jax.experimental.pallas import tpu as pltpu
from jax.sharding import PartitionSpec as P

STEPS = 2
BEND_SCALE = 0.5
HEUN_STEP = 0.3
HALO = 4
ORDERS = 4
MESH = pl.DeviceIdType.MESH


def shifted(parts, order, distance):
    n = distance
    result = parts[order - 1]
    factor = None
    for back in range(1, order):
        factor = n if factor is None else factor * (n + (back - 1.0)) / back
        result = result + factor * parts[order - 1 - back]
    return result


def bend_kernel(
    slabs, groups, depth, total_rows, scaling, x_ref, y_ref, r_ref, ox_ref, oy_ref,
    ext, edge_out, edge, local, total, arrived, final, outgoing, sums,
    base, middle, rho, source, density, pull, heads,
    own_sem, halo_send, halo_recv, edge_send, edge_recv, scan_send, scan_recv, last_send, last_recv,
):
    gx = lax.axis_index("gx")
    gz = lax.axis_index("gz")
    length, width = x_ref.shape
    w = width // 2
    margin = HALO * depth
    tiles = length // depth // 8 + 1
    fields = (x_ref, y_ref, r_ref)
    lane = lax.broadcasted_iota(jnp.int32, (8, w), 1)
    sub = lax.broadcasted_iota(jnp.int32, (8, w), 0)
    first_lane, last_lane = lane == 0, lane == w - 1

    def own_copy(a, h):
        return pltpu.make_async_copy(
            fields[a].at[:, pl.ds(h * w, w)], ext.at[a, h, pl.ds(margin, length)], own_sem.at[a, h]
        )

    for a in range(3):
        for h in range(2):
            own_copy(a, h).start()

    bits = slabs.bit_length() - 1
    half = lax.rem(gz, 2)
    sibling = gz + 1 - 2 * half

    def partner(bit):
        size = 1 << bit
        return gz + size - 2 * size * lax.rem(gz // size, 2)

    barrier = pltpu.get_barrier_semaphore()

    def greet(device):
        pl.semaphore_signal(barrier, inc=1, device_id=device, device_id_type=MESH)

    for bit in range(bits):
        greet((partner(bit), gx))
    other = gz + 2 * half - 1
    paired = (other >= 0) & (other < slabs)
    pl.when(paired)(lambda: greet((other, gx)))
    pl.when(gx > 0)(lambda: greet((gz, gx - 1)))
    pl.when(gx < groups - 1)(lambda: greet((gz, gx + 1)))
    peers = bits + paired.astype(jnp.int32) + (gx > 0).astype(jnp.int32) + (gx < groups - 1).astype(jnp.int32)
    pl.semaphore_wait(barrier, peers)

    def halo_copy(a, side, h):
        return pltpu.make_async_remote_copy(
            src_ref=fields[a].at[pl.ds(0 if side == 0 else length - margin, margin), pl.ds(h * w, w)],
            dst_ref=ext.at[a, h, pl.ds(margin + length if side == 0 else 0, margin)],
            send_sem=halo_send.at[a, side, h],
            recv_sem=halo_recv.at[a, side, h],
            device_id=(gz, gx - 1 + 2 * side),
            device_id_type=MESH,
        )

    def halo_start(side):
        for a in range(3):
            for h in range(2):
                halo_copy(a, side, h).start()

    def halo_land(side):
        for a in range(3):
            for h in range(2):
                halo_copy(a, side, h).wait_recv()

    def halo_clear(side):
        ext[:, :, pl.ds(margin + length if side == 0 else 0, margin)] = jnp.zeros((3, 2, margin, w), jnp.float32)

    pl.when(gx > 0)(lambda: halo_start(0))
    pl.when(gx < groups - 1)(lambda: halo_start(1))
    for a in range(3):
        for h in range(2):
            own_copy(a, h).wait()
    pl.when(gx < groups - 1)(lambda: halo_land(0))
    pl.when(gx == groups - 1)(lambda: halo_clear(0))
    pl.when(gx > 0)(lambda: halo_land(1))
    pl.when(gx == 0)(lambda: halo_clear(1))

    def coefficients(t):
        place = gx * (length // depth) - HALO + sub * tiles + t
        inside = ((place >= 0) & (place < total_rows)).astype(jnp.float32)
        curve = BEND_SCALE * (2.0 * (place.astype(jnp.float32) + 0.5) / total_rows - 1.0)
        return (0.5 * HEUN_STEP * scaling) * inside, HEUN_STEP * curve * inside

    def halves(v):
        return [v[:, :w], v[:, w:]]

    def beside_y(v):
        a, b = v
        ua, ub = pltpu.roll(a, w - 1, 1), pltpu.roll(b, w - 1, 1)
        da, db = pltpu.roll(a, 1, 1), pltpu.roll(b, 1, 1)
        up = [jnp.where(last_lane, ub, ua), jnp.where(last_lane, 0.0, ub)]
        down = [jnp.where(first_lane, 0.0, da), jnp.where(first_lane, da, db)]
        return up, down

    def wrap(ref, *index):
        ref[(*index, 0)] = pltpu.roll(ref[(*index, tiles)], 1, 0)
        ref[(*index, tiles + 1)] = pltpu.roll(ref[(*index, 1)], 7, 0)

    def laplace(ref, index, t):
        v = halves(ref[(*index, t + 1)])
        before, after = halves(ref[(*index, t)]), halves(ref[(*index, t + 2)])
        up, down = beside_y(v)
        return v, [(b + a) + (u + d) - 4.0 * c for a, b, c, u, d in zip(after, before, v, up, down)]

    def gradients(ref, index, t):
        v = halves(ref[(*index, t + 1)])
        before, after = halves(ref[(*index, t)]), halves(ref[(*index, t + 2)])
        up, down = beside_y(v)
        return [[a - b for a, b in zip(after, before)], [u - d for u, d in zip(up, down)]]

    def put(ref, index, value):
        ref[(*index, slice(None), slice(0, w))] = value[0]
        ref[(*index, slice(None), slice(w, width))] = value[1]

    def edge_copy(g):
        count = 3 if g < 2 else 2
        return pltpu.make_async_remote_copy(
            src_ref=edge_out.at[g, pl.ds(0, count)],
            dst_ref=edge.at[g, pl.ds(0, count)],
            send_sem=edge_send.at[g],
            recv_sem=edge_recv.at[g],
            device_id=(gz + 1, gx),
            device_id_type=MESH,
        )

    def edge_start(g):
        pl.when(gz < slabs - 1)(lambda: edge_copy(g).start())

    def tile_sums(t, _):
        for a in range(3):
            for h in range(2):
                cols = pl.ds(h * w, w)
                acc = [jnp.zeros((8, w), jnp.float32) for _ in range(ORDERS)]
                for z in range(depth):
                    step = ext[a, h, pl.ds(t * depth + z, 8, stride=tiles * depth), :]
                    if a == 2:
                        rho[z, t + 1, :, cols] = step
                    else:
                        base[a, z, t + 1, :, cols] = step
                    back = depth - 1 - z
                    if back < (2 if a == 2 else HALO):
                        edge_out[back, a, t, :, cols] = step
                    for m in range(ORDERS):
                        acc[m] = acc[m] + step
                        step = acc[m]
                for m in range(ORDERS):
                    local[h, m, a, t] = acc[m]
        return 0

    lax.fori_loop(0, tiles, tile_sums, 0)

    def scan_copy(stage, m):
        if stage == 0:
            source = local.at[1 - half, m]
        else:
            source = total.at[stage - 1, m]
        return pltpu.make_async_remote_copy(
            src_ref=source,
            dst_ref=arrived.at[stage, m],
            send_sem=scan_send.at[stage, m],
            recv_sem=scan_recv.at[stage, m],
            device_id=(partner(stage), gx),
            device_id_type=MESH,
        )

    def last_copy(m):
        return pltpu.make_async_remote_copy(
            src_ref=outgoing.at[m],
            dst_ref=final.at[m],
            send_sem=last_send.at[m],
            recv_sem=last_recv.at[m],
            device_id=(sibling, gx),
            device_id_type=MESH,
        )

    for m in range(ORDERS):
        scan_copy(0, m).start()
    edge_start(0)

    lower = []
    for m in range(ORDERS):
        scan_copy(0, m).wait_recv()
        mine, theirs = local[half, m], arrived[0, m]
        lower.append(jnp.where(half == 0, mine, theirs))
        total[0, m] = shifted(lower, m + 1, float(depth)) + jnp.where(half == 0, theirs, mine)
        if bits == 2:
            pl.when(partner(1) > gz)(lambda: scan_copy(1, m).start())
        else:
            scan_copy(1, m).start()

    prefix = [jnp.zeros_like(local[0, 0])] * ORDERS
    lows = [[] for _ in range(bits)]
    adds = [[] for _ in range(bits)]

    def scan_step(bit, m):
        size = 1 << bit
        is_upper = lax.rem(gz // size, 2)
        last = bit == bits - 1
        distance = ((lax.rem(gz, size) - half) * depth).astype(jnp.float32)
        if last:
            pl.when(is_upper == 1)(lambda: scan_copy(bit, m).wait_recv())

            def clear():
                arrived[bit, m] = jnp.zeros_like(arrived[bit, m])

            pl.when(is_upper == 0)(clear)
        else:
            scan_copy(bit, m).wait_recv()
        theirs = arrived[bit, m]
        adds[bit].append(theirs)
        if not last:
            mine = total[bit - 1, m]
            lows[bit].append(jnp.where(is_upper == 0, mine, theirs))
            high = jnp.where(is_upper == 0, theirs, mine)
            total[bit, m] = shifted(lows[bit], m + 1, float(depth * size)) + high
            if bit + 1 == bits - 1:
                pl.when(partner(bit + 1) > gz)(lambda: scan_copy(bit + 1, m).start())
            else:
                scan_copy(bit + 1, m).start()
        prefix[m] = prefix[m] + is_upper.astype(jnp.float32) * shifted(adds[bit], m + 1, distance)
        if last:
            even = prefix[m]
            odd = shifted(prefix, m + 1, float(depth)) + lower[m]
            sums[half, m] = jnp.where(half == 0, even, odd)
            outgoing[m] = jnp.where(half == 0, odd, even)
            last_copy(m).start()

    low, high = (-3, -2, -1, 0), (4, 3, 2, 1)
    first = (0, 8, 14, 18)

    def at(n, m):
        return first[n] + m - low[n]

    def pull_planes(orders):
        def tile(t, _):
            for m in orders:
                for f, g in enumerate(gradients(density, (m + 1,), t)):
                    put(pull, (f, m + 1, t), g)
            return 0

        lax.fori_loop(0, tiles, tile, 0)

    def gather_heads(g):
        last_copy(g).wait_recv()
        sums[1 - half, g] = final[g]
        pl.when(gz > 0)(lambda: edge_copy(g).wait_recv())

        def clear():
            edge[g] = jnp.zeros_like(edge[g])

        pl.when(gz == 0)(clear)

        def tile(t, _):
            for f in range(2):
                put(heads, (f, at(0, g + 1), t + 1), [sums[0, g, f, t], sums[1, g, f, t]])
                p = [edge[i, f, t] for i in range(g + 1)]
                if g == 0:
                    difference = p[0]
                elif g == 1:
                    difference = p[0] - p[1]
                elif g == 2:
                    difference = p[0] - 2.0 * p[1] + p[2]
                else:
                    difference = p[0] - 3.0 * (p[1] - p[2]) - p[3]
                heads[f, at(0, -g), t + 1] = difference
            put(density, (g + 2, t + 1), [sums[0, g, 2, t], sums[1, g, 2, t]])
            if g == 1:
                density[1, t + 1] = edge[0, 2, t]
            if g == 2:
                density[0, t + 1] = edge[0, 2, t] - edge[1, 2, t]
            return 0

        lax.fori_loop(0, tiles, tile, 0)
        fresh = [g + 1] + ([1 - g] if g in (1, 2) else [])
        for m in fresh:
            wrap(density, m + 1)
        for f in range(2):
            wrap(heads, f, at(0, g + 1))
            wrap(heads, f, at(0, -g))
        pull_planes(fresh)
        for n in range(1, g + 1):
            def raise_tile(t, _, n=n):
                c, k = coefficients(t)
                for f in range(2):
                    for m in (g + 1 - n, n - g):
                        _, force = laplace(heads, (f, at(n - 1, m + 1)), t)
                        q = halves(pull[f, m + 2, t])
                        now = halves(heads[f, at(n - 1, m), t + 1])
                        less = halves(heads[f, at(n - 1, m - 1), t + 1])
                        new = [v + c * (p - s) - k * d for v, p, s, d in zip(now, force, q, less)]
                        if n == 2:
                            old = halves(heads[f, at(0, m), t + 1])
                            new = [0.5 * (o + e) for o, e in zip(old, new)]
                        put(heads, (f, at(n, m), t + 1), new)
                return 0

            lax.fori_loop(0, tiles, raise_tile, 0)
            for f in range(2):
                for m in (g + 1 - n, n - g):
                    wrap(heads, f, at(n, m))

    def source_tile(t, _):
        for z in range(depth):
            for f, g in enumerate(gradients(rho, (z,), t)):
                put(source, (f, z, t), g)
        return 0

    def out_copy(f, h):
        return pltpu.make_async_copy(
            ext.at[f, h, pl.ds(margin, length)], (ox_ref, oy_ref)[f].at[:, pl.ds(h * w, w)], own_sem.at[f, h]
        )

    def level(n, f):
        origin, target = (base, middle) if n % 2 == 0 else (middle, base)

        def level_tile(t, _):
            c, k = coefficients(t)
            _, acc = laplace(heads, (f, at(n, 1)), t)
            acc = [q - s for q, s in zip(acc, halves(pull[f, 2, t]))]
            behind = halves(heads[f, at(n, 0), t + 1])
            for z in range(depth):
                v, force = laplace(origin, (f, z), t)
                g = halves(source[f, z, t])
                acc = [p + (q - s) for p, q, s in zip(acc, force, g)]
                new = [e + c * p + k * (b - e) for e, p, b in zip(v, acc, behind)]
                if n % 2 == 1:
                    new = [0.5 * (o + e) for o, e in zip(halves(base[f, z, t + 1]), new)]
                if n == 2 * STEPS - 1:
                    rows = pl.ds(t * depth + z, 8, stride=tiles * depth)
                    for h in range(2):
                        ext[f, h, rows, :] = new[h]
                else:
                    put(target, (f, z, t + 1), new)
                behind = v
            return 0

        lax.fori_loop(0, tiles, level_tile, 0)
        if n < 2 * STEPS - 1:
            for z in range(depth):
                wrap(target, f, z)
        else:
            for h in range(2):
                out_copy(f, h).start()

    for z in range(depth):
        wrap(rho, z)
        wrap(base, 0, z)
        wrap(base, 1, z)
    lax.fori_loop(0, tiles, source_tile, 0)

    for slot in range(1, bits + ORDERS - 1):
        for bit in range(1, bits):
            if 0 <= slot - bit < ORDERS:
                scan_step(bit, slot - bit)
                if bit == 1 and slot < ORDERS:
                    edge_start(slot)
        if slot == bits:
            gather_heads(0)
            level(0, 0)
        if slot == bits + 1:
            level(0, 1)
    for n in range(1, 2 * STEPS):
        gather_heads(n)
        for f in range(2):
            level(n, f)

    def edge_sent():
        for g in range(HALO):
            edge_copy(g).wait_send()

    pl.when(gz < slabs - 1)(edge_sent)

    def halo_sent(side):
        for a in range(3):
            for h in range(2):
                halo_copy(a, side, h).wait_send()

    pl.when(gx > 0)(lambda: halo_sent(0))
    pl.when(gx < groups - 1)(lambda: halo_sent(1))
    for m in range(ORDERS):
        last_copy(m).wait_send()
        for bit in range(bits):
            if bit == bits - 1:
                pl.when(partner(bit) > gz)(lambda: scan_copy(bit, m).wait_send())
            else:
                scan_copy(bit, m).wait_send()
    for f in range(2):
        for h in range(2):
            out_copy(f, h).wait()


def shards(slabs, groups, field_x, field_y, density):
    rows, depth, width = field_x.shape
    tiles = rows // 8 + 1
    length, margin = rows * depth, HALO * depth
    bits = slabs.bit_length() - 1
    f32 = jnp.float32
    anywhere = pl.BlockSpec(memory_space=pl.ANY)
    dma = pltpu.SemaphoreType.DMA
    chunk = (ORDERS, 3, tiles, 8, width // 2)
    plane = (tiles + 2, 8, width)
    result = jax.ShapeDtypeStruct((length, width), f32)
    new_x, new_y = pl.pallas_call(
        functools.partial(
            bend_kernel, slabs, groups, depth, rows * groups, 1.0 / math.sqrt(depth * slabs)
        ),
        out_shape=(result, result),
        in_specs=[anywhere] * 3,
        out_specs=[anywhere] * 2,
        scratch_shapes=[
            pltpu.VMEM((3, 2, length + 2 * margin, width // 2), f32),
            pltpu.VMEM((HALO, 3, tiles, 8, width), f32),
            pltpu.VMEM((HALO, 3, tiles, 8, width), f32),
            pltpu.VMEM((2,) + chunk, f32),
            pltpu.VMEM((max(bits - 1, 1),) + chunk, f32),
            pltpu.VMEM((bits,) + chunk, f32),
            pltpu.VMEM(chunk, f32),
            pltpu.VMEM(chunk, f32),
            pltpu.VMEM((2,) + chunk, f32),
            pltpu.VMEM((2, depth) + plane, f32),
            pltpu.VMEM((2, depth) + plane, f32),
            pltpu.VMEM((depth,) + plane, f32),
            pltpu.VMEM((2, depth, tiles, 8, width), f32),
            pltpu.VMEM((ORDERS + 2,) + plane, f32),
            pltpu.VMEM((2, ORDERS + 2, tiles, 8, width), f32),
            pltpu.VMEM((2, 20) + plane, f32),
            dma((3, 2)),
            dma((3, 2, 2)),
            dma((3, 2, 2)),
            dma((HALO,)),
            dma((HALO,)),
            dma((bits, ORDERS)),
            dma((bits, ORDERS)),
            dma((ORDERS,)),
            dma((ORDERS,)),
        ],
        compiler_params=pltpu.CompilerParams(
            collective_id=0, has_side_effects=True, vmem_limit_bytes=62 * 1024 * 1024
        ),
        name="bend",
    )(*[v.reshape(length, width) for v in (field_x, field_y, density)])
    return new_x.reshape(field_x.shape), new_y.reshape(field_x.shape)


def solution(mesh):
    spec = P("gx", "gz", None)
    return jax.shard_map(
        functools.partial(shards, mesh.shape["gz"], mesh.shape["gx"]),
        mesh=mesh,
        in_specs=(spec, spec, spec),
        out_specs=(spec, spec),
        check_vma=False,
    )
```

```python
import functools
import math

import jax
import jax.numpy as jnp
from jax import lax
from jax.experimental import pallas as pl
from jax.experimental.pallas import tpu as pltpu
from jax.sharding import PartitionSpec as P

STEPS = 2
BEND_SCALE = 0.5
HEUN_STEP = 0.3
HALO = 4
ORDERS = 4
MESH = pl.DeviceIdType.MESH


def shifted(parts, order, distance):
    n = distance
    result = parts[order - 1]
    factor = None
    for back in range(1, order):
        factor = n if factor is None else factor * (n + (back - 1.0)) / back
        result = result + factor * parts[order - 1 - back]
    return result


def bend_kernel(
    slabs, groups, depth, total_rows, scaling, x_ref, y_ref, r_ref, ox_ref, oy_ref,
    ext, edge_out, edge, passing, local, total, arrived, final, outgoing, sums,
    base, middle, rho, source, density, pull, heads,
    own_sem, halo_send, halo_recv, edge_send, edge_recv, pass_send, pass_recv, scan_send, scan_recv, last_send, last_recv,
):
    gx = lax.axis_index("gx")
    gz = lax.axis_index("gz")
    length, width = x_ref.shape
    w = width // 2
    margin = HALO * depth
    tiles = length // depth // 8 + 1
    fields = (x_ref, y_ref, r_ref)
    lane = lax.broadcasted_iota(jnp.int32, (8, w), 1)
    sub = lax.broadcasted_iota(jnp.int32, (8, w), 0)
    first_lane, last_lane = lane == 0, lane == w - 1

    def own_copy(a, h):
        return pltpu.make_async_copy(
            fields[a].at[:, pl.ds(h * w, w)], ext.at[a, h, pl.ds(margin, length)], own_sem.at[a, h]
        )

    for a in range(3):
        for h in range(2):
            own_copy(a, h).start()

    bits = slabs.bit_length() - 1
    half = lax.rem(gz, 2)
    sibling = gz + 1 - 2 * half

    def partner(bit):
        size = 1 << bit
        return gz + size - 2 * size * lax.rem(gz // size, 2)

    barrier = pltpu.get_barrier_semaphore()

    def greet(device):
        pl.semaphore_signal(barrier, inc=1, device_id=device, device_id_type=MESH)

    for bit in range(bits):
        greet((partner(bit), gx))
    other = gz + 2 * half - 1
    paired = (other >= 0) & (other < slabs)
    pl.when(paired)(lambda: greet((other, gx)))
    if slabs % 8 == 0:
        place = lax.rem(gz, 8)
        crossing = (place == 4) | (place == 7)
        pl.when(crossing)(lambda: greet((gz + jnp.where(place == 4, 3, -3), gx)))
    else:
        crossing = gz < 0
    pl.when(gx > 0)(lambda: greet((gz, gx - 1)))
    pl.when(gx < groups - 1)(lambda: greet((gz, gx + 1)))
    peers = bits + paired.astype(jnp.int32) + crossing.astype(jnp.int32) + (gx > 0).astype(jnp.int32) + (gx < groups - 1).astype(jnp.int32)
    pl.semaphore_wait(barrier, peers)

    def halo_copy(a, side, h):
        return pltpu.make_async_remote_copy(
            src_ref=fields[a].at[pl.ds(0 if side == 0 else length - margin, margin), pl.ds(h * w, w)],
            dst_ref=ext.at[a, h, pl.ds(margin + length if side == 0 else 0, margin)],
            send_sem=halo_send.at[a, side, h],
            recv_sem=halo_recv.at[a, side, h],
            device_id=(gz, gx - 1 + 2 * side),
            device_id_type=MESH,
        )

    def halo_start(side):
        for a in range(3):
            for h in range(2):
                halo_copy(a, side, h).start()

    def halo_land(side):
        for a in range(3):
            for h in range(2):
                halo_copy(a, side, h).wait_recv()

    def halo_clear(side):
        ext[:, :, pl.ds(margin + length if side == 0 else 0, margin)] = jnp.zeros((3, 2, margin, w), jnp.float32)

    pl.when(gx > 0)(lambda: halo_start(0))
    pl.when(gx < groups - 1)(lambda: halo_start(1))
    for a in range(3):
        for h in range(2):
            own_copy(a, h).wait()
    pl.when(gx < groups - 1)(lambda: halo_land(0))
    pl.when(gx == groups - 1)(lambda: halo_clear(0))
    pl.when(gx > 0)(lambda: halo_land(1))
    pl.when(gx == 0)(lambda: halo_clear(1))

    def coefficients(t):
        place = gx * (length // depth) - HALO + sub * tiles + t
        inside = ((place >= 0) & (place < total_rows)).astype(jnp.float32)
        curve = BEND_SCALE * (2.0 * (place.astype(jnp.float32) + 0.5) / total_rows - 1.0)
        return (0.5 * HEUN_STEP * scaling) * inside, HEUN_STEP * curve * inside

    def halves(v):
        return [v[:, :w], v[:, w:]]

    def beside_y(v):
        a, b = v
        ua, ub = pltpu.roll(a, w - 1, 1), pltpu.roll(b, w - 1, 1)
        da, db = pltpu.roll(a, 1, 1), pltpu.roll(b, 1, 1)
        up = [jnp.where(last_lane, ub, ua), jnp.where(last_lane, 0.0, ub)]
        down = [jnp.where(first_lane, 0.0, da), jnp.where(first_lane, da, db)]
        return up, down

    def wrap(ref, *index):
        ref[(*index, 0)] = pltpu.roll(ref[(*index, tiles)], 1, 0)
        ref[(*index, tiles + 1)] = pltpu.roll(ref[(*index, 1)], 7, 0)

    def laplace(ref, index, t):
        v = halves(ref[(*index, t + 1)])
        before, after = halves(ref[(*index, t)]), halves(ref[(*index, t + 2)])
        up, down = beside_y(v)
        return v, [(b + a) + (u + d) - 4.0 * c for a, b, c, u, d in zip(after, before, v, up, down)]

    def gradients(ref, index, t):
        v = halves(ref[(*index, t + 1)])
        before, after = halves(ref[(*index, t)]), halves(ref[(*index, t + 2)])
        up, down = beside_y(v)
        return [[a - b for a, b in zip(after, before)], [u - d for u, d in zip(up, down)]]

    def put(ref, index, value):
        ref[(*index, slice(None), slice(0, w))] = value[0]
        ref[(*index, slice(None), slice(w, width))] = value[1]

    if slabs % 8 == 0:
        via = lax.rem(gz, 8) == 3
        relay = lax.rem(gz, 8) == 7
    else:
        via = relay = gz < 0
    direct = (gz < slabs - 1) & jnp.logical_not(via)

    def edge_copy(g, hop=0):
        part = pl.ds(0, 3 if g < 2 else 2)
        source, target, device = (
            (edge_out, edge, gz + 1), (edge_out, passing, gz + 4), (passing, edge, gz - 3)
        )[hop]
        return pltpu.make_async_remote_copy(
            src_ref=source.at[g, part],
            dst_ref=target.at[g, part],
            send_sem=(pass_send if hop == 2 else edge_send).at[g],
            recv_sem=(pass_recv if hop == 1 else edge_recv).at[g],
            device_id=(device, gx),
            device_id_type=MESH,
        )

    def edge_start(g):
        pl.when(direct)(lambda: edge_copy(g).start())

    def via_start():
        for g in range(HALO):
            edge_copy(g, 1).start()

    def edge_pass(g):
        def go():
            edge_copy(g, 1).wait_recv()
            edge_copy(g, 2).start()

        pl.when(relay)(go)

    def tile_sums(t, _):
        for a in range(3):
            for h in range(2):
                cols = pl.ds(h * w, w)
                acc = [jnp.zeros((8, w), jnp.float32) for _ in range(ORDERS)]
                for z in range(depth):
                    step = ext[a, h, pl.ds(t * depth + z, 8, stride=tiles * depth), :]
                    if a == 2:
                        rho[z, t + 1, :, cols] = step
                    else:
                        base[a, z, t + 1, :, cols] = step
                    back = depth - 1 - z
                    if back < (2 if a == 2 else HALO):
                        edge_out[back, a, t, :, cols] = step
                    for m in range(ORDERS):
                        acc[m] = acc[m] + step
                        step = acc[m]
                for m in range(ORDERS):
                    local[h, m, a, t] = acc[m]
        return 0

    lax.fori_loop(0, tiles, tile_sums, 0)

    def scan_copy(stage, m):
        if stage == 0:
            source = local.at[1 - half, m]
        else:
            source = total.at[stage - 1, m]
        return pltpu.make_async_remote_copy(
            src_ref=source,
            dst_ref=arrived.at[stage, m],
            send_sem=scan_send.at[stage, m],
            recv_sem=scan_recv.at[stage, m],
            device_id=(partner(stage), gx),
            device_id_type=MESH,
        )

    def last_copy(m):
        return pltpu.make_async_remote_copy(
            src_ref=outgoing.at[m],
            dst_ref=final.at[m],
            send_sem=last_send.at[m],
            recv_sem=last_recv.at[m],
            device_id=(sibling, gx),
            device_id_type=MESH,
        )

    for m in range(ORDERS):
        scan_copy(0, m).start()
    edge_start(0)
    pl.when(via)(via_start)

    lower = []
    for m in range(ORDERS):
        scan_copy(0, m).wait_recv()
        mine, theirs = local[half, m], arrived[0, m]
        lower.append(jnp.where(half == 0, mine, theirs))
        total[0, m] = shifted(lower, m + 1, float(depth)) + jnp.where(half == 0, theirs, mine)
        if bits == 2:
            pl.when(partner(1) > gz)(lambda: scan_copy(1, m).start())
        else:
            scan_copy(1, m).start()

    prefix = [jnp.zeros_like(local[0, 0])] * ORDERS
    lows = [[] for _ in range(bits)]
    adds = [[] for _ in range(bits)]

    def scan_step(bit, m):
        size = 1 << bit
        is_upper = lax.rem(gz // size, 2)
        last = bit == bits - 1
        distance = ((lax.rem(gz, size) - half) * depth).astype(jnp.float32)
        if last:
            pl.when(is_upper == 1)(lambda: scan_copy(bit, m).wait_recv())

            def clear():
                arrived[bit, m] = jnp.zeros_like(arrived[bit, m])

            pl.when(is_upper == 0)(clear)
        else:
            scan_copy(bit, m).wait_recv()
        theirs = arrived[bit, m]
        adds[bit].append(theirs)
        if not last:
            mine = total[bit - 1, m]
            lows[bit].append(jnp.where(is_upper == 0, mine, theirs))
            high = jnp.where(is_upper == 0, theirs, mine)
            total[bit, m] = shifted(lows[bit], m + 1, float(depth * size)) + high
            if bit + 1 == bits - 1:
                pl.when(partner(bit + 1) > gz)(lambda: scan_copy(bit + 1, m).start())
            else:
                scan_copy(bit + 1, m).start()
        prefix[m] = prefix[m] + is_upper.astype(jnp.float32) * shifted(adds[bit], m + 1, distance)
        if last:
            even = prefix[m]
            odd = shifted(prefix, m + 1, float(depth)) + lower[m]
            sums[half, m] = jnp.where(half == 0, even, odd)
            outgoing[m] = jnp.where(half == 0, odd, even)
            last_copy(m).start()

    low, high = (-3, -2, -1, 0), (4, 3, 2, 1)
    first = (0, 8, 14, 18)

    def at(n, m):
        return first[n] + m - low[n]

    def pull_planes(orders):
        def tile(t, _):
            for m in orders:
                for f, g in enumerate(gradients(density, (m + 1,), t)):
                    put(pull, (f, m + 1, t), g)
            return 0

        lax.fori_loop(0, tiles, tile, 0)

    def gather_heads(g):
        last_copy(g).wait_recv()
        sums[1 - half, g] = final[g]
        pl.when(gz > 0)(lambda: edge_copy(g).wait_recv())

        def clear():
            edge[g] = jnp.zeros_like(edge[g])

        pl.when(gz == 0)(clear)

        def tile(t, _):
            for f in range(2):
                put(heads, (f, at(0, g + 1), t + 1), [sums[0, g, f, t], sums[1, g, f, t]])
                p = [edge[i, f, t] for i in range(g + 1)]
                if g == 0:
                    difference = p[0]
                elif g == 1:
                    difference = p[0] - p[1]
                elif g == 2:
                    difference = p[0] - 2.0 * p[1] + p[2]
                else:
                    difference = p[0] - 3.0 * (p[1] - p[2]) - p[3]
                heads[f, at(0, -g), t + 1] = difference
            put(density, (g + 2, t + 1), [sums[0, g, 2, t], sums[1, g, 2, t]])
            if g == 1:
                density[1, t + 1] = edge[0, 2, t]
            if g == 2:
                density[0, t + 1] = edge[0, 2, t] - edge[1, 2, t]
            return 0

        lax.fori_loop(0, tiles, tile, 0)
        fresh = [g + 1] + ([1 - g] if g in (1, 2) else [])
        for m in fresh:
            wrap(density, m + 1)
        for f in range(2):
            wrap(heads, f, at(0, g + 1))
            wrap(heads, f, at(0, -g))
        pull_planes(fresh)
        for n in range(1, g + 1):
            def raise_tile(t, _, n=n):
                c, k = coefficients(t)
                for f in range(2):
                    for m in (g + 1 - n, n - g):
                        _, force = laplace(heads, (f, at(n - 1, m + 1)), t)
                        q = halves(pull[f, m + 2, t])
                        now = halves(heads[f, at(n - 1, m), t + 1])
                        less = halves(heads[f, at(n - 1, m - 1), t + 1])
                        new = [v + c * (p - s) - k * d for v, p, s, d in zip(now, force, q, less)]
                        if n == 2:
                            old = halves(heads[f, at(0, m), t + 1])
                            new = [0.5 * (o + e) for o, e in zip(old, new)]
                        put(heads, (f, at(n, m), t + 1), new)
                return 0

            lax.fori_loop(0, tiles, raise_tile, 0)
            for f in range(2):
                for m in (g + 1 - n, n - g):
                    wrap(heads, f, at(n, m))

    def source_tile(t, _):
        for z in range(depth):
            for f, g in enumerate(gradients(rho, (z,), t)):
                put(source, (f, z, t), g)
        return 0

    def out_copy(f, h):
        return pltpu.make_async_copy(
            ext.at[f, h, pl.ds(margin, length)], (ox_ref, oy_ref)[f].at[:, pl.ds(h * w, w)], own_sem.at[f, h]
        )

    def level(n, f):
        origin, target = (base, middle) if n % 2 == 0 else (middle, base)

        def level_tile(t, _):
            c, k = coefficients(t)
            _, acc = laplace(heads, (f, at(n, 1)), t)
            acc = [q - s for q, s in zip(acc, halves(pull[f, 2, t]))]
            behind = halves(heads[f, at(n, 0), t + 1])
            for z in range(depth):
                v, force = laplace(origin, (f, z), t)
                g = halves(source[f, z, t])
                acc = [p + (q - s) for p, q, s in zip(acc, force, g)]
                new = [e + c * p + k * (b - e) for e, p, b in zip(v, acc, behind)]
                if n % 2 == 1:
                    new = [0.5 * (o + e) for o, e in zip(halves(base[f, z, t + 1]), new)]
                if n == 2 * STEPS - 1:
                    rows = pl.ds(t * depth + z, 8, stride=tiles * depth)
                    for h in range(2):
                        ext[f, h, rows, :] = new[h]
                else:
                    put(target, (f, z, t + 1), new)
                behind = v
            return 0

        lax.fori_loop(0, tiles, level_tile, 0)
        if n < 2 * STEPS - 1:
            for z in range(depth):
                wrap(target, f, z)
        else:
            for h in range(2):
                out_copy(f, h).start()

    for z in range(depth):
        wrap(rho, z)
        wrap(base, 0, z)
        wrap(base, 1, z)
    lax.fori_loop(0, tiles, source_tile, 0)

    def advance(n):
        gather_heads(n)
        for f in range(2):
            level(n, f)

    for slot in range(1, bits + ORDERS - 1):
        for bit in range(1, bits):
            if 0 <= slot - bit < ORDERS:
                scan_step(bit, slot - bit)
                if bit == 1:
                    edge_pass(slot - 1)
                    if slot < ORDERS:
                        edge_start(slot)
        if slot >= bits:
            advance(slot - bits)
    advance(ORDERS - 1)

    def edge_sent():
        for g in range(HALO):
            edge_copy(g).wait_send()

    pl.when(gz < slabs - 1)(edge_sent)

    def edge_passed():
        for g in range(HALO):
            edge_copy(g, 2).wait_send()

    pl.when(relay)(edge_passed)

    def halo_sent(side):
        for a in range(3):
            for h in range(2):
                halo_copy(a, side, h).wait_send()

    pl.when(gx > 0)(lambda: halo_sent(0))
    pl.when(gx < groups - 1)(lambda: halo_sent(1))
    for m in range(ORDERS):
        last_copy(m).wait_send()
        for bit in range(bits):
            if bit == bits - 1:
                pl.when(partner(bit) > gz)(lambda: scan_copy(bit, m).wait_send())
            else:
                scan_copy(bit, m).wait_send()
    for f in range(2):
        for h in range(2):
            out_copy(f, h).wait()


def shards(slabs, groups, field_x, field_y, density):
    rows, depth, width = field_x.shape
    tiles = rows // 8 + 1
    length, margin = rows * depth, HALO * depth
    bits = slabs.bit_length() - 1
    f32 = jnp.float32
    anywhere = pl.BlockSpec(memory_space=pl.ANY)
    dma = pltpu.SemaphoreType.DMA
    chunk = (ORDERS, 3, tiles, 8, width // 2)
    plane = (tiles + 2, 8, width)
    result = jax.ShapeDtypeStruct((length, width), f32)
    new_x, new_y = pl.pallas_call(
        functools.partial(
            bend_kernel, slabs, groups, depth, rows * groups, 1.0 / math.sqrt(depth * slabs)
        ),
        out_shape=(result, result),
        in_specs=[anywhere] * 3,
        out_specs=[anywhere] * 2,
        scratch_shapes=[
            pltpu.VMEM((3, 2, length + 2 * margin, width // 2), f32),
            pltpu.VMEM((HALO, 3, tiles, 8, width), f32),
            pltpu.VMEM((HALO, 3, tiles, 8, width), f32),
            pltpu.VMEM((HALO, 3, tiles, 8, width), f32),
            pltpu.VMEM((2,) + chunk, f32),
            pltpu.VMEM((max(bits - 1, 1),) + chunk, f32),
            pltpu.VMEM((bits,) + chunk, f32),
            pltpu.VMEM(chunk, f32),
            pltpu.VMEM(chunk, f32),
            pltpu.VMEM((2,) + chunk, f32),
            pltpu.VMEM((2, depth) + plane, f32),
            pltpu.VMEM((2, depth) + plane, f32),
            pltpu.VMEM((depth,) + plane, f32),
            pltpu.VMEM((2, depth, tiles, 8, width), f32),
            pltpu.VMEM((ORDERS + 2,) + plane, f32),
            pltpu.VMEM((2, ORDERS + 2, tiles, 8, width), f32),
            pltpu.VMEM((2, 20) + plane, f32),
            dma((3, 2)),
            dma((3, 2, 2)),
            dma((3, 2, 2)),
            dma((HALO,)),
            dma((HALO,)),
            dma((HALO,)),
            dma((HALO,)),
            dma((bits, ORDERS)),
            dma((bits, ORDERS)),
            dma((ORDERS,)),
            dma((ORDERS,)),
        ],
        compiler_params=pltpu.CompilerParams(
            collective_id=0, has_side_effects=True, vmem_limit_bytes=62 * 1024 * 1024
        ),
        name="bend",
    )(*[v.reshape(length, width) for v in (field_x, field_y, density)])
    return new_x.reshape(field_x.shape), new_y.reshape(field_x.shape)


def solution(mesh):
    spec = P("gx", "gz", None)
    return jax.shard_map(
        functools.partial(shards, mesh.shape["gz"], mesh.shape["gx"]),
        mesh=mesh,
        in_specs=(spec, spec, spec),
        out_specs=(spec, spec),
        check_vma=False,
    )
```

```python
import functools
import math

import jax
import jax.numpy as jnp
from jax import lax
from jax.experimental import pallas as pl
from jax.experimental.pallas import tpu as pltpu
from jax.sharding import PartitionSpec as P

STEPS = 2
BEND_SCALE = 0.5
HEUN_STEP = 0.3
HALO = 4
ORDERS = 4
MESH = pl.DeviceIdType.MESH


def shifted(parts, order, distance):
    n = distance
    result = parts[order - 1]
    factor = None
    for back in range(1, order):
        factor = n if factor is None else factor * (n + (back - 1.0)) / back
        result = result + factor * parts[order - 1 - back]
    return result


def bend_kernel(
    slabs, groups, depth, total_rows, scaling, x_ref, y_ref, r_ref, ox_ref, oy_ref,
    ext, edge_out, edge, passing, local, total, arrived, final, outgoing, sums,
    base, middle, rho, source, density, pull, heads,
    own_sem, halo_send, halo_recv, edge_send, edge_recv, pass_send, pass_recv, scan_send, scan_recv, last_send, last_recv,
):
    gx = lax.axis_index("gx")
    gz = lax.axis_index("gz")
    length, width = x_ref.shape
    w = width // 2
    margin = HALO * depth
    tiles = length // depth // 8 + 1
    fields = (x_ref, y_ref, r_ref)
    lane = lax.broadcasted_iota(jnp.int32, (8, w), 1)
    sub = lax.broadcasted_iota(jnp.int32, (8, w), 0)
    first_lane, last_lane = lane == 0, lane == w - 1

    def own_copy(a, h):
        return pltpu.make_async_copy(
            fields[a].at[:, pl.ds(h * w, w)], ext.at[a, h, pl.ds(margin, length)], own_sem.at[a, h]
        )

    for a in range(3):
        for h in range(2):
            own_copy(a, h).start()

    bits = slabs.bit_length() - 1
    half = lax.rem(gz, 2)
    sibling = gz + 1 - 2 * half

    def partner(bit):
        size = 1 << bit
        return gz + size - 2 * size * lax.rem(gz // size, 2)

    barrier = pltpu.get_barrier_semaphore()

    def greet(device):
        pl.semaphore_signal(barrier, inc=1, device_id=device, device_id_type=MESH)

    for bit in range(bits):
        greet((partner(bit), gx))
    other = gz + 2 * half - 1
    paired = (other >= 0) & (other < slabs)
    pl.when(paired)(lambda: greet((other, gx)))
    if slabs % 8 == 0:
        place = lax.rem(gz, 8)
        crossing = (place == 4) | (place == 7)
        pl.when(crossing)(lambda: greet((gz + jnp.where(place == 4, 3, -3), gx)))
    else:
        crossing = gz < 0
    pl.when(gx > 0)(lambda: greet((gz, gx - 1)))
    pl.when(gx < groups - 1)(lambda: greet((gz, gx + 1)))
    peers = bits + paired.astype(jnp.int32) + crossing.astype(jnp.int32) + (gx > 0).astype(jnp.int32) + (gx < groups - 1).astype(jnp.int32)
    pl.semaphore_wait(barrier, peers)

    def halo_copy(a, side, h):
        return pltpu.make_async_remote_copy(
            src_ref=fields[a].at[pl.ds(0 if side == 0 else length - margin, margin), pl.ds(h * w, w)],
            dst_ref=ext.at[a, h, pl.ds(margin + length if side == 0 else 0, margin)],
            send_sem=halo_send.at[a, side, h],
            recv_sem=halo_recv.at[a, side, h],
            device_id=(gz, gx - 1 + 2 * side),
            device_id_type=MESH,
        )

    def halo_start(side):
        for a in range(3):
            for h in range(2):
                halo_copy(a, side, h).start()

    def halo_land(side):
        for a in range(3):
            for h in range(2):
                halo_copy(a, side, h).wait_recv()

    def halo_clear(side):
        ext[:, :, pl.ds(margin + length if side == 0 else 0, margin)] = jnp.zeros((3, 2, margin, w), jnp.float32)

    pl.when(gx > 0)(lambda: halo_start(0))
    pl.when(gx < groups - 1)(lambda: halo_start(1))
    for a in range(3):
        for h in range(2):
            own_copy(a, h).wait()
    pl.when(gx < groups - 1)(lambda: halo_land(0))
    pl.when(gx == groups - 1)(lambda: halo_clear(0))
    pl.when(gx > 0)(lambda: halo_land(1))
    pl.when(gx == 0)(lambda: halo_clear(1))

    def coefficients(t):
        place = gx * (length // depth) - HALO + sub * tiles + t
        inside = ((place >= 0) & (place < total_rows)).astype(jnp.float32)
        curve = BEND_SCALE * (2.0 * (place.astype(jnp.float32) + 0.5) / total_rows - 1.0)
        return (0.5 * HEUN_STEP * scaling) * inside, HEUN_STEP * curve * inside

    def halves(v):
        return [v[:, :w], v[:, w:]]

    def beside_y(v):
        a, b = v
        ua, ub = pltpu.roll(a, w - 1, 1), pltpu.roll(b, w - 1, 1)
        da, db = pltpu.roll(a, 1, 1), pltpu.roll(b, 1, 1)
        up = [jnp.where(last_lane, ub, ua), jnp.where(last_lane, 0.0, ub)]
        down = [jnp.where(first_lane, 0.0, da), jnp.where(first_lane, da, db)]
        return up, down

    def wrap(ref, *index):
        ref[(*index, 0)] = pltpu.roll(ref[(*index, tiles)], 1, 0)
        ref[(*index, tiles + 1)] = pltpu.roll(ref[(*index, 1)], 7, 0)

    def laplace(ref, index, t):
        v = halves(ref[(*index, t + 1)])
        before, after = halves(ref[(*index, t)]), halves(ref[(*index, t + 2)])
        up, down = beside_y(v)
        return v, [(b + a) + (u + d) - 4.0 * c for a, b, c, u, d in zip(after, before, v, up, down)]

    def gradients(ref, index, t):
        v = halves(ref[(*index, t + 1)])
        before, after = halves(ref[(*index, t)]), halves(ref[(*index, t + 2)])
        up, down = beside_y(v)
        return [[a - b for a, b in zip(after, before)], [u - d for u, d in zip(up, down)]]

    def put(ref, index, value):
        ref[(*index, slice(None), slice(0, w))] = value[0]
        ref[(*index, slice(None), slice(w, width))] = value[1]

    if slabs % 8 == 0:
        via = lax.rem(gz, 8) == 3
        relay = lax.rem(gz, 8) == 7
    else:
        via = relay = gz < 0
    direct = (gz < slabs - 1) & jnp.logical_not(via)

    def edge_copy(g, hop=0):
        part = pl.ds(0, 3 if g < 2 else 2)
        source, target, device = (
            (edge_out, edge, gz + 1), (edge_out, passing, gz + 4), (passing, edge, gz - 3)
        )[hop]
        return pltpu.make_async_remote_copy(
            src_ref=source.at[g, part],
            dst_ref=target.at[g, part],
            send_sem=(pass_send if hop == 2 else edge_send).at[g],
            recv_sem=(pass_recv if hop == 1 else edge_recv).at[g],
            device_id=(device, gx),
            device_id_type=MESH,
        )

    def edge_start(g):
        pl.when(direct)(lambda: edge_copy(g).start())

    def via_start():
        for g in range(HALO):
            edge_copy(g, 1).start()

    def edge_pass(g):
        def go():
            edge_copy(g, 1).wait_recv()
            edge_copy(g, 2).start()

        pl.when(relay)(go)

    def tile_sums(t, _):
        for a in range(3):
            for h in range(2):
                cols = pl.ds(h * w, w)
                acc = [jnp.zeros((8, w), jnp.float32) for _ in range(ORDERS)]
                for z in range(depth):
                    step = ext[a, h, pl.ds(t * depth + z, 8, stride=tiles * depth), :]
                    if a == 2:
                        rho[z, t + 1, :, cols] = step
                    else:
                        base[a, z, t + 1, :, cols] = step
                    back = depth - 1 - z
                    if back < (2 if a == 2 else HALO):
                        edge_out[back, a, t, :, cols] = step
                    for m in range(ORDERS):
                        acc[m] = acc[m] + step
                        step = acc[m]
                for m in range(ORDERS):
                    local[h, m, a, t] = acc[m]
        return 0

    lax.fori_loop(0, tiles, tile_sums, 0, unroll=3 if tiles % 3 == 0 else 1)

    def scan_copy(stage, m):
        if stage == 0:
            source = local.at[1 - half, m]
        else:
            source = total.at[stage - 1, m]
        return pltpu.make_async_remote_copy(
            src_ref=source,
            dst_ref=arrived.at[stage, m],
            send_sem=scan_send.at[stage, m],
            recv_sem=scan_recv.at[stage, m],
            device_id=(partner(stage), gx),
            device_id_type=MESH,
        )

    def needs(bit, device):
        above = lax.rem(device // (1 << bit), 2) == 1
        if bit == bits - 1:
            return above
        if bit == bits - 2 and bit > 0:
            return above | (lax.rem(device // (1 << (bits - 1)), 2) == 0)
        return None

    def scan_start(bit, m):
        useful = needs(bit, partner(bit))
        if useful is None:
            scan_copy(bit, m).start()
        else:
            pl.when(useful)(lambda: scan_copy(bit, m).start())

    def scan_sent(bit, m):
        useful = needs(bit, partner(bit))
        if useful is None:
            scan_copy(bit, m).wait_send()
        else:
            pl.when(useful)(lambda: scan_copy(bit, m).wait_send())

    def last_copy(m):
        return pltpu.make_async_remote_copy(
            src_ref=outgoing.at[m],
            dst_ref=final.at[m],
            send_sem=last_send.at[m],
            recv_sem=last_recv.at[m],
            device_id=(sibling, gx),
            device_id_type=MESH,
        )

    for m in range(ORDERS):
        scan_copy(0, m).start()
    edge_start(0)
    pl.when(via)(via_start)

    lower = []
    for m in range(ORDERS):
        scan_copy(0, m).wait_recv()
        mine, theirs = local[half, m], arrived[0, m]
        lower.append(jnp.where(half == 0, mine, theirs))
        total[0, m] = shifted(lower, m + 1, float(depth)) + jnp.where(half == 0, theirs, mine)
        scan_start(1, m)

    prefix = [jnp.zeros_like(local[0, 0])] * ORDERS
    lows = [[] for _ in range(bits)]
    adds = [[] for _ in range(bits)]

    def scan_step(bit, m):
        size = 1 << bit
        is_upper = lax.rem(gz // size, 2)
        last = bit == bits - 1
        distance = ((lax.rem(gz, size) - half) * depth).astype(jnp.float32)
        needed = needs(bit, gz)
        if needed is None:
            scan_copy(bit, m).wait_recv()
        else:
            pl.when(needed)(lambda: scan_copy(bit, m).wait_recv())

            def clear():
                arrived[bit, m] = jnp.zeros_like(arrived[bit, m])

            pl.when(jnp.logical_not(needed))(clear)
        theirs = arrived[bit, m]
        adds[bit].append(theirs)
        if not last:
            mine = total[bit - 1, m]
            lows[bit].append(jnp.where(is_upper == 0, mine, theirs))
            high = jnp.where(is_upper == 0, theirs, mine)
            total[bit, m] = shifted(lows[bit], m + 1, float(depth * size)) + high
            scan_start(bit + 1, m)
        prefix[m] = prefix[m] + is_upper.astype(jnp.float32) * shifted(adds[bit], m + 1, distance)
        if last:
            even = prefix[m]
            odd = shifted(prefix, m + 1, float(depth)) + lower[m]
            sums[half, m] = jnp.where(half == 0, even, odd)
            outgoing[m] = jnp.where(half == 0, odd, even)
            last_copy(m).start()

    low, high = (-3, -2, -1, 0), (4, 3, 2, 1)
    first = (0, 8, 14, 18)

    def at(n, m):
        return first[n] + m - low[n]

    def pull_planes(orders):
        def tile(t, _):
            for m in orders:
                for f, g in enumerate(gradients(density, (m + 1,), t)):
                    put(pull, (f, m + 1, t), g)
            return 0

        lax.fori_loop(0, tiles, tile, 0, unroll=3 if tiles % 3 == 0 else 1)

    def gather_heads(g):
        last_copy(g).wait_recv()
        sums[1 - half, g] = final[g]
        pl.when(gz > 0)(lambda: edge_copy(g).wait_recv())

        def clear():
            edge[g] = jnp.zeros_like(edge[g])

        pl.when(gz == 0)(clear)

        def tile(t, _):
            for f in range(2):
                put(heads, (f, at(0, g + 1), t + 1), [sums[0, g, f, t], sums[1, g, f, t]])
                p = [edge[i, f, t] for i in range(g + 1)]
                if g == 0:
                    difference = p[0]
                elif g == 1:
                    difference = p[0] - p[1]
                elif g == 2:
                    difference = p[0] - 2.0 * p[1] + p[2]
                else:
                    difference = p[0] - 3.0 * (p[1] - p[2]) - p[3]
                heads[f, at(0, -g), t + 1] = difference
            put(density, (g + 2, t + 1), [sums[0, g, 2, t], sums[1, g, 2, t]])
            if g == 1:
                density[1, t + 1] = edge[0, 2, t]
            if g == 2:
                density[0, t + 1] = edge[0, 2, t] - edge[1, 2, t]
            return 0

        lax.fori_loop(0, tiles, tile, 0, unroll=3 if tiles % 3 == 0 else 1)
        fresh = [g + 1] + ([1 - g] if g in (1, 2) else [])
        for m in fresh:
            wrap(density, m + 1)
        for f in range(2):
            wrap(heads, f, at(0, g + 1))
            wrap(heads, f, at(0, -g))
        pull_planes(fresh)
        for n in range(1, g + 1):
            def raise_tile(t, _, n=n):
                c, k = coefficients(t)
                for f in range(2):
                    for m in (g + 1 - n, n - g):
                        _, force = laplace(heads, (f, at(n - 1, m + 1)), t)
                        q = halves(pull[f, m + 2, t])
                        now = halves(heads[f, at(n - 1, m), t + 1])
                        less = halves(heads[f, at(n - 1, m - 1), t + 1])
                        new = [v + c * (p - s) - k * d for v, p, s, d in zip(now, force, q, less)]
                        if n == 2:
                            old = halves(heads[f, at(0, m), t + 1])
                            new = [0.5 * (o + e) for o, e in zip(old, new)]
                        put(heads, (f, at(n, m), t + 1), new)
                return 0

            lax.fori_loop(0, tiles, raise_tile, 0, unroll=3 if tiles % 3 == 0 else 1)
            for f in range(2):
                for m in (g + 1 - n, n - g):
                    wrap(heads, f, at(n, m))

    def source_tile(t, _):
        for z in range(depth):
            for f, g in enumerate(gradients(rho, (z,), t)):
                put(source, (f, z, t), g)
        return 0

    def out_copy(f, h):
        return pltpu.make_async_copy(
            ext.at[f, h, pl.ds(margin, length)], (ox_ref, oy_ref)[f].at[:, pl.ds(h * w, w)], own_sem.at[f, h]
        )

    def level(n, f):
        origin, target = (base, middle) if n % 2 == 0 else (middle, base)

        def level_tile(t, _):
            c, k = coefficients(t)
            _, acc = laplace(heads, (f, at(n, 1)), t)
            acc = [q - s for q, s in zip(acc, halves(pull[f, 2, t]))]
            behind = halves(heads[f, at(n, 0), t + 1])
            for z in range(depth):
                v, force = laplace(origin, (f, z), t)
                g = halves(source[f, z, t])
                acc = [p + (q - s) for p, q, s in zip(acc, force, g)]
                new = [e + c * p + k * (b - e) for e, p, b in zip(v, acc, behind)]
                if n % 2 == 1:
                    new = [0.5 * (o + e) for o, e in zip(halves(base[f, z, t + 1]), new)]
                if n == 2 * STEPS - 1:
                    rows = pl.ds(t * depth + z, 8, stride=tiles * depth)
                    for h in range(2):
                        ext[f, h, rows, :] = new[h]
                else:
                    put(target, (f, z, t + 1), new)
                behind = v
            return 0

        lax.fori_loop(0, tiles, level_tile, 0, unroll=True)
        if n < 2 * STEPS - 1:
            for z in range(depth):
                wrap(target, f, z)
        else:
            for h in range(2):
                out_copy(f, h).start()

    for z in range(depth):
        wrap(rho, z)
        wrap(base, 0, z)
        wrap(base, 1, z)
    lax.fori_loop(0, tiles, source_tile, 0, unroll=3 if tiles % 3 == 0 else 1)

    def advance(n):
        gather_heads(n)
        for f in range(2):
            level(n, f)

    for slot in range(1, bits + ORDERS - 1):
        for bit in range(1, bits):
            if 0 <= slot - bit < ORDERS:
                scan_step(bit, slot - bit)
                if bit == 1:
                    edge_pass(slot - 1)
                    if slot < ORDERS:
                        edge_start(slot)
        if slot >= bits:
            advance(slot - bits)
    advance(ORDERS - 1)

    def edge_sent():
        for g in range(HALO):
            edge_copy(g).wait_send()

    pl.when(gz < slabs - 1)(edge_sent)

    def edge_passed():
        for g in range(HALO):
            edge_copy(g, 2).wait_send()

    pl.when(relay)(edge_passed)

    def halo_sent(side):
        for a in range(3):
            for h in range(2):
                halo_copy(a, side, h).wait_send()

    pl.when(gx > 0)(lambda: halo_sent(0))
    pl.when(gx < groups - 1)(lambda: halo_sent(1))
    for m in range(ORDERS):
        last_copy(m).wait_send()
        for bit in range(bits):
            scan_sent(bit, m)
    for f in range(2):
        for h in range(2):
            out_copy(f, h).wait()


def shards(slabs, groups, field_x, field_y, density):
    rows, depth, width = field_x.shape
    tiles = rows // 8 + 1
    length, margin = rows * depth, HALO * depth
    bits = slabs.bit_length() - 1
    f32 = jnp.float32
    anywhere = pl.BlockSpec(memory_space=pl.ANY)
    dma = pltpu.SemaphoreType.DMA
    chunk = (ORDERS, 3, tiles, 8, width // 2)
    plane = (tiles + 2, 8, width)
    result = jax.ShapeDtypeStruct((length, width), f32)
    new_x, new_y = pl.pallas_call(
        functools.partial(
            bend_kernel, slabs, groups, depth, rows * groups, 1.0 / math.sqrt(depth * slabs)
        ),
        out_shape=(result, result),
        in_specs=[anywhere] * 3,
        out_specs=[anywhere] * 2,
        scratch_shapes=[
            pltpu.VMEM((3, 2, length + 2 * margin, width // 2), f32),
            pltpu.VMEM((HALO, 3, tiles, 8, width), f32),
            pltpu.VMEM((HALO, 3, tiles, 8, width), f32),
            pltpu.VMEM((HALO, 3, tiles, 8, width), f32),
            pltpu.VMEM((2,) + chunk, f32),
            pltpu.VMEM((max(bits - 1, 1),) + chunk, f32),
            pltpu.VMEM((bits,) + chunk, f32),
            pltpu.VMEM(chunk, f32),
            pltpu.VMEM(chunk, f32),
            pltpu.VMEM((2,) + chunk, f32),
            pltpu.VMEM((2, depth) + plane, f32),
            pltpu.VMEM((2, depth) + plane, f32),
            pltpu.VMEM((depth,) + plane, f32),
            pltpu.VMEM((2, depth, tiles, 8, width), f32),
            pltpu.VMEM((ORDERS + 2,) + plane, f32),
            pltpu.VMEM((2, ORDERS + 2, tiles, 8, width), f32),
            pltpu.VMEM((2, 20) + plane, f32),
            dma((3, 2)),
            dma((3, 2, 2)),
            dma((3, 2, 2)),
            dma((HALO,)),
            dma((HALO,)),
            dma((HALO,)),
            dma((HALO,)),
            dma((bits, ORDERS)),
            dma((bits, ORDERS)),
            dma((ORDERS,)),
            dma((ORDERS,)),
        ],
        compiler_params=pltpu.CompilerParams(
            collective_id=0, has_side_effects=True, vmem_limit_bytes=62 * 1024 * 1024
        ),
        name="bend",
    )(*[v.reshape(length, width) for v in (field_x, field_y, density)])
    return new_x.reshape(field_x.shape), new_y.reshape(field_x.shape)


def solution(mesh):
    spec = P("gx", "gz", None)
    return jax.shard_map(
        functools.partial(shards, mesh.shape["gz"], mesh.shape["gx"]),
        mesh=mesh,
        in_specs=(spec, spec, spec),
        out_specs=(spec, spec),
        check_vma=False,
    )
```
